128 devices in a mesh: rep: 32 (over x, y, z_lo), tp: 4 (over z_hi, core).
Axes of the slice: x: 4, y: 4, z: 4 (z_hi: 2, z_lo: 2; z = z_hi * 2 + z_lo), core: 2. Of those that a mesh axis runs over, the one named last changes fastest.
Arguments:
- step_index: int32 [1], replicated, may hold values from 0 to 5
- inputs: bfloat16 [16384, 5120], P(('rep', 'tp')), may hold values from -6 to 6
- grad_out: bfloat16 [16384, 5120], P(('rep', 'tp')), may hold values from -6 to 6
- params: float32 [32, 3, 224, 5120], P('rep', None, 'tp'), may hold values from -0.078125 to 0.078125
- first_moment: float32 [32, 3, 224, 5120], P('rep', None, 'tp'), may hold values from -24 to 24
- second_moment: float32 [32, 3, 224, 5120], P('rep', None, 'tp'), may hold values from 16 to 1024
Outputs:
- new_params: float32 [32, 3, 224, 5120], P('rep', None, 'tp')
- new_first: float32 [32, 3, 224, 5120], P('rep', None, 'tp')
- new_second: float32 [32, 3, 224, 5120], P('rep', None, 'tp')
- input_grad: bfloat16 [16384, 5120], P(('rep', 'tp'))
The draws below stay inside these ranges and needn't reach their ends.
All inputs are finite; a program needn't handle non-finite values.
Results may differ from the reference program's by a relative error of at most 0.0072.
Values may be sent and summed in bfloat16 or wider, within the bound.
A program may use at most 128 MiB of HBM per device.

```python
import math
import jax
import jax.numpy as jnp
from jax import lax

D = 5120
TOK = 512
HID = 224
TOKENS = 16384
N_REP = 32


def levels(own_key, extent, shards, least, largest):
    def one(dim, parts):
        heights = jax.random.uniform(jax.random.fold_in(jax.random.fold_in(own_key, 6), dim), (parts,), jnp.float32, least / len(shards), largest / len(shards))
        return jnp.repeat(jnp.exp(heights), extent[dim] // parts).reshape((-1,) + (1,) * (len(extent) - dim - 1))

    factor_of = one(*shards[0])
    for cut in shards[1:]:
        factor_of = factor_of * one(*cut)
    return factor_of


def scatter_about(stream_key, dims, scale, reach, split=(), kind=jnp.bfloat16):
    result = scale * jax.random.normal(stream_key, dims, jnp.float32)
    if split:
        result = result * levels(stream_key, dims, split, -0.22, 0.18)
    return jnp.clip(result, -reach, reach).astype(kind)


def setup_inputs(seed: int = 0) -> dict:
    seeds = jax.random.split(jax.random.key(seed), 7)
    step_index = jax.random.randint(seeds[0], (1,), 0, 6).astype(jnp.int32)
    inputs = scatter_about(seeds[1], (TOKENS, D), 1.0, 6.0, ((0, 128),))
    grad_out = scatter_about(seeds[2], (TOKENS, D), 1.0, 6.0, ((0, 128),))
    params = scatter_about(seeds[3], (N_REP, 3, HID, D), D ** -0.5, 0.078125, ((0, 32), (2, 4)), jnp.float32)
    first_moment = scatter_about(seeds[4], (N_REP, 3, HID, D), 4.0, 24.0, ((0, 32), (2, 4)), jnp.float32)
    second_moment = jnp.clip(jnp.exp(math.log(1024.0) - 4.158883 * jax.random.uniform(seeds[5], (N_REP, 3, HID, D), jnp.float32) ** levels(seeds[5], (N_REP, 3, HID, D), ((0, 32), (2, 4)), -0.2, 0.2)), 16.0, 1024.0)
    return dict(step_index=step_index, inputs=inputs, grad_out=grad_out, params=params, first_moment=first_moment, second_moment=second_moment)


def one_replica(item, step_index):
    inputs, grad_out, weights, first, second = item
    low = weights.astype(jnp.bfloat16)
    gate_w = low[0]
    up_w = low[1]
    down_w = low[2]
    pre_gate = jnp.dot(gate_w, inputs.T, preferred_element_type=jnp.float32)
    pre_up = jnp.dot(up_w, inputs.T, preferred_element_type=jnp.float32)
    back_hidden = jnp.dot(down_w, grad_out.T, preferred_element_type=jnp.float32)
    sigma = jax.nn.sigmoid(pre_gate)
    silu_val = sigma * pre_gate
    hidden = (silu_val * pre_up).astype(jnp.bfloat16)
    d_gate = (back_hidden * pre_up * sigma * (1.0 + pre_gate * (1.0 - sigma))).astype(jnp.bfloat16)
    d_up = (back_hidden * silu_val).astype(jnp.bfloat16)
    grads = jnp.stack([jnp.dot(d_gate, inputs, preferred_element_type=jnp.float32), jnp.dot(d_up, inputs, preferred_element_type=jnp.float32), jnp.dot(hidden, grad_out, preferred_element_type=jnp.float32)])
    input_grad = jnp.dot(d_gate.T, gate_w, preferred_element_type=jnp.float32) + jnp.dot(d_up.T, up_w, preferred_element_type=jnp.float32)
    count = (step_index[0] + 1).astype(jnp.float32)
    new_first = 0.9 * first + 0.1 * grads
    new_second = 0.95 * second + 0.05 * grads * grads
    fix_first = 1.0 - jnp.power(jnp.float32(0.9), count)
    fix_second = 1.0 - jnp.power(jnp.float32(0.95), count)
    update = new_first / fix_first / (jnp.sqrt(new_second / fix_second) + 1e-08)
    updated = weights - 0.01 * (update + 0.1 * weights)
    return (updated, new_first, new_second, input_grad.astype(jnp.bfloat16))

def reference(step_index, inputs, grad_out, params, first_moment, second_moment):
    x_all = inputs.reshape(N_REP, TOK, D)
    g_all = grad_out.reshape(N_REP, TOK, D)
    updated, new_first, new_second, input_grad = lax.map(lambda item: one_replica(item, step_index), (x_all, g_all, params, first_moment, second_moment))
    bits = N_REP.bit_length() - 1
    power = step_index[0] % bits
    distance = jnp.left_shift(jnp.int32(1), power.astype(jnp.int32))
    peer = jnp.roll(updated, distance, axis=0)
    new_params = 0.5 * (updated + peer)
    return (new_params, new_first, new_second, input_grad.reshape(TOKENS, D))
```

```python
import functools
import jax
import jax.numpy as jnp
from jax import lax
from jax.experimental import pallas as pl
from jax.experimental.pallas import tpu as pltpu
from jax.sharding import PartitionSpec as P

CHUNK = 512
HALF = CHUNK // 2
WIDE = CHUNK + HALF
SLAB = 16
LAG = 2
MESH = pl.DeviceIdType.MESH
BF16 = jnp.bfloat16
F32 = jnp.float32
NT = (((1,), (1,)), ((), ()))
NN = (((1,), (0,)), ((), ()))
TN = (((0,), (0,)), ((), ()))


def dot(a, b, dims):
    return lax.dot_general(a, b, dims, preferred_element_type=F32)


def window_kernel(
    by,
    scale_ref, x_ref, g_ref, p_ref, m_ref, v_ref,
    np_ref, nm_ref, nv_ref, ig_ref,
    xb, gb, pb, mb, vb, w_own, w_rem, g_send, g_recv, u_send, u_recv,
    ig_send, ig_recv, ig_out, acc_a, acc_b, grad,
    d_own, d_rem, h_own, h_rem,
    p_sem, m_sem, v_sem, x_sem, g_sem,
    xs_sem, xr_sem, gs_sem, gr_sem,
    ws_sem, wr_sem, ds_sem, dr_sem, us_sem, ur_sem, is_sem, ir_sem,
    po_sem, mo_sem, vo_sem, io_sem,
):
    n_rep = lax.axis_size("rep")
    rep = lax.axis_index("rep")
    tp = lax.axis_index("tp")
    core = lax.rem(tp, 2)
    z_peer = (rep, lax.rem(tp + 2, 4))
    twin = (rep, tp + 1 - 2 * core)
    after = (lax.rem(rep + by, n_rep), tp)
    before = (lax.rem(rep + n_rep - by, n_rep), tp)

    tok, width = x_ref.shape
    hid = p_ref.shape[2]
    pair = 2 * hid
    count = width // CHUNK
    mine = pl.multiple_of(core * tok, tok)
    other = pl.multiple_of((1 - core) * tok, tok)

    def parts(hbm, buf, j):
        whole = pl.ds(pl.multiple_of(j * CHUNK, CHUNK), CHUNK)
        left = pl.ds(pl.multiple_of(j * CHUNK, HALF), HALF)
        right = pl.ds(pl.multiple_of(j * CHUNK + HALF, HALF), HALF)
        return [
            (hbm.at[0, 0, :, whole], buf.at[j, pl.ds(0, hid), pl.ds(0, CHUNK)]),
            (hbm.at[0, 1, :, whole], buf.at[j, pl.ds(hid, hid), pl.ds(0, CHUNK)]),
            (hbm.at[0, 2, :, left], buf.at[j, pl.ds(0, hid), pl.ds(CHUNK, HALF)]),
            (hbm.at[0, 2, :, right], buf.at[j, pl.ds(hid, hid), pl.ds(CHUNK, HALF)]),
        ]

    def load(hbm, buf, sem, j):
        for a, b in parts(hbm, buf, j):
            pltpu.make_async_copy(a, b, sem.at[j]).start()

    def store(hbm, buf, sem, j):
        for a, b in parts(hbm, buf, j):
            pltpu.make_async_copy(b, a, sem.at[j]).start()

    def wait_chunk(buf, sem, j):
        pltpu.make_async_copy(buf.at[j], buf.at[j], sem.at[j]).wait()

    def cols(j):
        return pl.ds(pl.multiple_of(j * CHUNK, CHUNK), CHUNK)

    def tokens_in(hbm, buf, sem, j):
        return pltpu.make_async_copy(
            hbm.at[:, cols(j)], buf.at[j, pl.ds(mine, tok), :], sem.at[j])

    def tokens_over(hbm, buf, s_sem, r_sem, j):
        return pltpu.make_async_remote_copy(
            src_ref=hbm.at[:, cols(j)], dst_ref=buf.at[j, pl.ds(mine, tok), :],
            send_sem=s_sem.at[j], recv_sem=r_sem.at[j],
            device_id=twin, device_id_type=MESH)

    def send(src, dst, s_sem, r_sem, device, j):
        return pltpu.make_async_remote_copy(
            src_ref=src.at[j], dst_ref=dst.at[j],
            send_sem=s_sem.at[j], recv_sem=r_sem.at[j],
            device_id=device, device_id_type=MESH)

    def loop(body):
        def step(j, carry):
            body(j)
            return carry
        lax.fori_loop(0, count, step, 0)

    barrier = pltpu.get_barrier_semaphore()
    for device in (z_peer, twin, before):
        pl.semaphore_signal(barrier, inc=1, device_id=device, device_id_type=MESH)

    loop(lambda j: load(p_ref, pb, p_sem, j))

    def token_loads(j):
        tokens_in(x_ref, xb, x_sem, j).start()
        tokens_in(g_ref, gb, g_sem, j).start()

    loop(token_loads)
    pl.semaphore_wait(barrier, 3)

    def send_weights(j):
        wait_chunk(pb, p_sem, j)
        w_own[j] = pb[j].astype(BF16)
        send(w_own, w_rem, ws_sem, wr_sem, z_peer, j).start()
        tokens_over(x_ref, xb, xs_sem, xr_sem, j).start()
        tokens_over(g_ref, gb, gs_sem, gr_sem, j).start()

    loop(send_weights)

    def moment_loads(j):
        load(m_ref, mb, m_sem, j)
        load(v_ref, vb, v_sem, j)

    loop(moment_loads)

    def project(w, j):
        acc_a[...] += dot(w[j, :, pl.ds(0, CHUNK)], xb[j], NT)
        down = w[j, :, pl.ds(CHUNK, HALF)]
        top = dot(down[: hid + 8], gb[j, :, pl.ds(0, HALF)], NT)
        low = dot(down[hid - 8:], gb[j, :, pl.ds(HALF, HALF)], NT)
        acc_b[...] += top[:hid] + low[8:]

    def start_sums():
        acc_a[...] = jnp.zeros_like(acc_a)
        acc_b[...] = jnp.zeros_like(acc_b)

    def finish_hidden(d_ref, h_ref):
        pre_gate = acc_a[pl.ds(0, hid), :]
        pre_up = acc_a[pl.ds(hid, hid), :]
        back = acc_b[...]
        s = jax.nn.sigmoid(pre_gate)
        silu = s * pre_gate
        pad = jnp.zeros((8, 2 * tok), F32)
        h_ref[...] = jnp.concatenate([silu * pre_up, pad], axis=0).astype(BF16)
        d_gate = back * pre_up * s * (1.0 + pre_gate * (1.0 - s))
        d_ref[...] = jnp.concatenate([d_gate, back * silu], axis=0).astype(BF16)

    def project_own(j):
        tokens_in(x_ref, xb, x_sem, j).wait()
        tokens_in(g_ref, gb, g_sem, j).wait()
        tokens_over(x_ref, xb, xs_sem, xr_sem, j).wait_recv()
        tokens_over(g_ref, gb, gs_sem, gr_sem, j).wait_recv()
        project(w_own, j)

    start_sums()
    loop(project_own)
    finish_hidden(d_own, h_own)

    def project_rem(j):
        send(w_own, w_rem, ws_sem, wr_sem, z_peer, j).wait_recv()
        project(w_rem, j)

    start_sums()
    loop(project_rem)
    finish_hidden(d_rem, h_rem)

    def gradient(d_ref, h_ref, j):
        first = dot(d_ref[...], xb[j], NN)
        last = dot(h_ref[...], gb[j], NN)[:hid]
        return first, jnp.concatenate([last[:, :HALF], last[:, HALF:]], axis=0)

    def send_gradients(j):
        first, last = gradient(d_rem, h_rem, j)
        g_send[j, :, pl.ds(0, CHUNK)] = first.astype(BF16)
        g_send[j, :, pl.ds(CHUNK, HALF)] = last.astype(BF16)
        send(g_send, g_recv, ds_sem, dr_sem, z_peer, j).start()

    loop(send_gradients)

    def back_project(rows, j):
        return dot(d_own[:, pl.ds(rows, tok)], w_own[j, :, pl.ds(0, CHUNK)], TN) + dot(
            d_rem[:, pl.ds(rows, tok)], w_rem[j, :, pl.ds(0, CHUNK)], TN)

    scale_first = scale_ref[0]
    scale_second = scale_ref[1]

    def adam(j):
        first, last = gradient(d_own, h_own, j)
        grad[:, pl.ds(0, CHUNK)] = first
        grad[:, pl.ds(CHUNK, HALF)] = last
        send(g_send, g_recv, ds_sem, dr_sem, z_peer, j).wait_recv()
        wait_chunk(mb, m_sem, j)
        wait_chunk(vb, v_sem, j)

        def slab(i, carry):
            rows = pl.ds(pl.multiple_of(i * SLAB, SLAB), SLAB)
            gr = grad[rows, :] + g_recv[j, rows, :].astype(F32)
            first_new = 0.9 * mb[j, rows, :] + 0.1 * gr
            second_new = 0.95 * vb[j, rows, :] + 0.05 * gr * gr
            mb[j, rows, :] = first_new
            vb[j, rows, :] = second_new
            weights = pb[j, rows, :]
            update = first_new * scale_first / (jnp.sqrt(second_new * scale_second) + 1e-08)
            updated = weights - 0.01 * (update + 0.1 * weights)
            pb[j, rows, :] = updated
            u_send[j, rows, :] = updated.astype(BF16)
            return carry

        lax.fori_loop(0, pair // SLAB, slab, 0)

    def average(j):
        send(u_send, u_recv, us_sem, ur_sem, after, j).wait_recv()
        pb[j] = 0.5 * (pb[j] + u_recv[j].astype(F32))
        store(np_ref, pb, po_sem, j)

    def input_gradient(j):
        send(ig_send, ig_recv, is_sem, ir_sem, twin, j).wait_recv()
        ig_out[j] = (back_project(mine, j) + ig_recv[j]).astype(BF16)
        pltpu.make_async_copy(ig_out.at[j], ig_ref.at[:, cols(j)], io_sem.at[j]).start()

    def update_step(j):
        adam(j)
        send(u_send, u_recv, us_sem, ur_sem, after, j).start()
        store(nm_ref, mb, mo_sem, j)
        store(nv_ref, vb, vo_sem, j)
        ig_send[j] = back_project(other, j)
        send(ig_send, ig_recv, is_sem, ir_sem, twin, j).start()

        @pl.when(j >= 1)
        def _():
            input_gradient(j - 1)

        @pl.when(j >= LAG)
        def _():
            average(j - LAG)

    loop(update_step)
    input_gradient(count - 1)
    for j in range(count - LAG, count):
        average(j)

    def drain(j):
        send(w_own, w_rem, ws_sem, wr_sem, z_peer, j).wait_send()
        tokens_over(x_ref, xb, xs_sem, xr_sem, j).wait_send()
        tokens_over(g_ref, gb, gs_sem, gr_sem, j).wait_send()
        send(g_send, g_recv, ds_sem, dr_sem, z_peer, j).wait_send()
        send(u_send, u_recv, us_sem, ur_sem, after, j).wait_send()
        send(ig_send, ig_recv, is_sem, ir_sem, twin, j).wait_send()
        wait_chunk(pb, po_sem, j)
        wait_chunk(mb, mo_sem, j)
        wait_chunk(vb, vo_sem, j)
        pltpu.make_async_copy(ig_out.at[j], ig_ref.at[:, cols(j)], io_sem.at[j]).wait()

    loop(drain)


def window(by, collective_id, scales, inputs, grad_out, params, first, second):
    tok, width = inputs.shape
    hid = params.shape[2]
    pair = 2 * hid
    count = width // CHUNK
    anywhere = pl.BlockSpec(memory_space=pl.ANY)
    block = pltpu.VMEM((count, pair, WIDE), BF16)
    wide = pltpu.VMEM((count, pair, WIDE), F32)
    token = pltpu.VMEM((count, 2 * tok, CHUNK), BF16)
    partial = pltpu.VMEM((count, tok, CHUNK), F32)
    like = jax.ShapeDtypeStruct(params.shape, F32)
    return pl.pallas_call(
        functools.partial(window_kernel, by),
        out_shape=[like, like, like, jax.ShapeDtypeStruct(inputs.shape, BF16)],
        in_specs=[pl.BlockSpec(memory_space=pltpu.SMEM)] + [anywhere] * 5,
        out_specs=[anywhere] * 4,
        scratch_shapes=[token] * 2 + [wide] * 3 + [block] * 6 + [partial] * 2
        + [pltpu.VMEM((count, tok, CHUNK), BF16)]
        + [pltpu.VMEM((pair, 2 * tok), F32), pltpu.VMEM((hid, 2 * tok), F32)]
        + [pltpu.VMEM((pair, WIDE), F32)]
        + [pltpu.VMEM((pair, 2 * tok), BF16)] * 2
        + [pltpu.VMEM((hid + 8, 2 * tok), BF16)] * 2
        + [pltpu.SemaphoreType.DMA((count,))] * 21,
        compiler_params=pltpu.CompilerParams(
            collective_id=collective_id, has_side_effects=True,
            vmem_limit_bytes=56 * 2 ** 20),
        name=f"window_by_{by}",
    )(scales, inputs, grad_out, params, first, second)


def copy_kernel(n, *refs):
    sources, targets, sem = refs[:n], refs[n: 2 * n], refs[2 * n]
    copies = []
    for source, target in zip(sources, targets):
        if len(source.shape) == 4:
            pieces = [(source.at[0, i], target.at[0, i]) for i in range(source.shape[1])]
        else:
            pieces = [(source, target)]
        for a, b in pieces:
            copies.append(pltpu.make_async_copy(a, b, sem.at[len(copies)]))
    for copy in copies:
        copy.start()
    for copy in copies:
        copy.wait()


def hand_over(arrays):
    n = len(arrays)
    anywhere = pl.BlockSpec(memory_space=pl.ANY)
    return pl.pallas_call(
        functools.partial(copy_kernel, n),
        out_shape=[jax.ShapeDtypeStruct(a.shape, a.dtype) for a in arrays],
        in_specs=[anywhere] * n,
        out_specs=[anywhere] * n,
        scratch_shapes=[pltpu.SemaphoreType.DMA((3 * n,))],
        name="hand_over",
    )(*arrays)


def make_branch(bit):

    def run(*values):
        return tuple(hand_over(window(1 << bit, bit, *values)))

    return run


def per_device(step_index, inputs, grad_out, params, first_moment, second_moment):
    bits = lax.axis_size("rep").bit_length() - 1
    count_now = (step_index[0] + 1).astype(F32)
    fixes = 1.0 - jnp.power(jnp.array([0.9, 0.95], F32), count_now)
    branches = [make_branch(bit) for bit in range(bits)]
    return lax.switch(
        step_index[0] % bits, branches, 1.0 / fixes,
        inputs, grad_out, params, first_moment, second_moment)


def solution(mesh):
    return jax.shard_map(
        per_device,
        mesh=mesh,
        in_specs=(
            P(),
            P(("rep", "tp"), None),
            P(("rep", "tp"), None),
            P("rep", None, "tp", None),
            P("rep", None, "tp", None),
            P("rep", None, "tp", None),
        ),
        out_specs=(
            P("rep", None, "tp", None),
            P("rep", None, "tp", None),
            P("rep", None, "tp", None),
            P(("rep", "tp"), None),
        ),
        check_vma=False,
    )
```

```python
import functools
import jax
import jax.numpy as jnp
from jax import lax
from jax.experimental import pallas as pl
from jax.experimental.pallas import tpu as pltpu
from jax.sharding import PartitionSpec as P

CHUNK = 512
HALF = CHUNK // 2
WIDE = CHUNK + HALF
SLAB = 16
LAG = 2
MESH = pl.DeviceIdType.MESH
BF16 = jnp.bfloat16
F32 = jnp.float32
NT = (((1,), (1,)), ((), ()))
NN = (((1,), (0,)), ((), ()))
TN = (((0,), (0,)), ((), ()))


def dot(a, b, dims):
    return lax.dot_general(a, b, dims, preferred_element_type=F32)


def window_kernel(
    by,
    scale_ref, x_ref, g_ref, p_ref, m_ref, v_ref,
    np_ref, nm_ref, nv_ref, ig_ref,
    xb, gb, pb, mb, vb, w_own, w_rem, g_send, g_recv, u_send, u_recv,
    ig_send, ig_recv, ig_out, acc_a, acc_b, grad,
    d_own, d_rem, h_own, h_rem,
    p_sem, m_sem, v_sem, x_sem, g_sem,
    xs_sem, xr_sem, gs_sem, gr_sem,
    ws_sem, wr_sem, ds_sem, dr_sem, us_sem, ur_sem, is_sem, ir_sem,
    po_sem, mo_sem, vo_sem, io_sem,
):
    n_rep = lax.axis_size("rep")
    rep = lax.axis_index("rep")
    tp = lax.axis_index("tp")
    core = lax.rem(tp, 2)
    z_peer = (rep, lax.rem(tp + 2, 4))
    twin = (rep, tp + 1 - 2 * core)
    after = (lax.rem(rep + by, n_rep), tp)
    before = (lax.rem(rep + n_rep - by, n_rep), tp)

    tok, width = x_ref.shape
    hid = p_ref.shape[2]
    pair = 2 * hid
    count = width // CHUNK
    mine = pl.multiple_of(core * tok, tok)
    other = pl.multiple_of((1 - core) * tok, tok)

    def parts(hbm, buf, j):
        whole = pl.ds(pl.multiple_of(j * CHUNK, CHUNK), CHUNK)
        left = pl.ds(pl.multiple_of(j * CHUNK, HALF), HALF)
        right = pl.ds(pl.multiple_of(j * CHUNK + HALF, HALF), HALF)
        return [
            (hbm.at[0, 0, :, whole], buf.at[j, pl.ds(0, hid), pl.ds(0, CHUNK)]),
            (hbm.at[0, 1, :, whole], buf.at[j, pl.ds(hid, hid), pl.ds(0, CHUNK)]),
            (hbm.at[0, 2, :, left], buf.at[j, pl.ds(0, hid), pl.ds(CHUNK, HALF)]),
            (hbm.at[0, 2, :, right], buf.at[j, pl.ds(hid, hid), pl.ds(CHUNK, HALF)]),
        ]

    def load(hbm, buf, sem, j):
        for a, b in parts(hbm, buf, j):
            pltpu.make_async_copy(a, b, sem.at[j]).start()

    def store(hbm, buf, sem, j):
        for a, b in parts(hbm, buf, j):
            pltpu.make_async_copy(b, a, sem.at[j]).start()

    def wait_chunk(buf, sem, j):
        pltpu.make_async_copy(buf.at[j], buf.at[j], sem.at[j]).wait()

    def cols(j):
        return pl.ds(pl.multiple_of(j * CHUNK, CHUNK), CHUNK)

    def tokens_in(hbm, buf, sem, j):
        return pltpu.make_async_copy(
            hbm.at[:, cols(j)], buf.at[j, pl.ds(mine, tok), :], sem.at[j])

    def tokens_over(hbm, buf, s_sem, r_sem, j):
        return pltpu.make_async_remote_copy(
            src_ref=hbm.at[:, cols(j)], dst_ref=buf.at[j, pl.ds(mine, tok), :],
            send_sem=s_sem.at[j], recv_sem=r_sem.at[j],
            device_id=twin, device_id_type=MESH)

    def send(src, dst, s_sem, r_sem, device, j):
        return pltpu.make_async_remote_copy(
            src_ref=src.at[j], dst_ref=dst.at[j],
            send_sem=s_sem.at[j], recv_sem=r_sem.at[j],
            device_id=device, device_id_type=MESH)

    def loop(body):
        def step(j, carry):
            body(j)
            return carry
        lax.fori_loop(0, count, step, 0)

    barrier = pltpu.get_barrier_semaphore()
    for device in (z_peer, twin, before):
        pl.semaphore_signal(barrier, inc=1, device_id=device, device_id_type=MESH)

    loop(lambda j: load(p_ref, pb, p_sem, j))

    def token_loads(j):
        tokens_in(x_ref, xb, x_sem, j).start()
        tokens_in(g_ref, gb, g_sem, j).start()

    loop(token_loads)
    pl.semaphore_wait(barrier, 3)

    def send_weights(j):
        wait_chunk(pb, p_sem, j)
        w_own[j] = pb[j].astype(BF16)
        send(w_own, w_rem, ws_sem, wr_sem, z_peer, j).start()
        tokens_over(x_ref, xb, xs_sem, xr_sem, j).start()
        tokens_over(g_ref, gb, gs_sem, gr_sem, j).start()

    loop(send_weights)

    def moment_loads(j):
        load(m_ref, mb, m_sem, j)
        load(v_ref, vb, v_sem, j)

    loop(moment_loads)

    def project(w, j):
        acc_a[...] += dot(w[j, :, pl.ds(0, CHUNK)], xb[j], NT)
        down = w[j, :, pl.ds(CHUNK, HALF)]
        top = dot(down[: hid + 8], gb[j, :, pl.ds(0, HALF)], NT)
        low = dot(down[hid - 8:], gb[j, :, pl.ds(HALF, HALF)], NT)
        acc_b[...] += top[:hid] + low[8:]

    def start_sums():
        acc_a[...] = jnp.zeros_like(acc_a)
        acc_b[...] = jnp.zeros_like(acc_b)

    def finish_hidden(d_ref, h_ref):
        pre_gate = acc_a[pl.ds(0, hid), :]
        pre_up = acc_a[pl.ds(hid, hid), :]
        back = acc_b[...]
        s = jax.nn.sigmoid(pre_gate)
        silu = s * pre_gate
        pad = jnp.zeros((8, 2 * tok), F32)
        h_ref[...] = jnp.concatenate([silu * pre_up, pad], axis=0).astype(BF16)
        d_gate = back * pre_up * s * (1.0 + pre_gate * (1.0 - s))
        d_ref[...] = jnp.concatenate([d_gate, back * silu], axis=0).astype(BF16)

    def project_own(j):
        tokens_in(x_ref, xb, x_sem, j).wait()
        tokens_in(g_ref, gb, g_sem, j).wait()
        tokens_over(x_ref, xb, xs_sem, xr_sem, j).wait_recv()
        tokens_over(g_ref, gb, gs_sem, gr_sem, j).wait_recv()
        project(w_own, j)

    start_sums()
    loop(project_own)
    finish_hidden(d_own, h_own)

    def project_rem(j):
        send(w_own, w_rem, ws_sem, wr_sem, z_peer, j).wait_recv()
        project(w_rem, j)

    start_sums()
    loop(project_rem)
    finish_hidden(d_rem, h_rem)

    def gradient(d_ref, h_ref, j):
        first = dot(d_ref[...], xb[j], NN)
        last = dot(h_ref[...], gb[j], NN)[:hid]
        return first, jnp.concatenate([last[:, :HALF], last[:, HALF:]], axis=0)

    def send_gradients(j):
        first, last = gradient(d_rem, h_rem, j)
        g_send[j, :, pl.ds(0, CHUNK)] = first.astype(BF16)
        g_send[j, :, pl.ds(CHUNK, HALF)] = last.astype(BF16)
        send(g_send, g_recv, ds_sem, dr_sem, z_peer, j).start()

    loop(send_gradients)

    def back_project(rows, j):
        return dot(d_own[:, pl.ds(rows, tok)], w_own[j, :, pl.ds(0, CHUNK)], TN) + dot(
            d_rem[:, pl.ds(rows, tok)], w_rem[j, :, pl.ds(0, CHUNK)], TN)

    scale_first = scale_ref[0]
    scale_second = scale_ref[1]

    def adam(j):
        first, last = gradient(d_own, h_own, j)
        grad[:, pl.ds(0, CHUNK)] = first
        grad[:, pl.ds(CHUNK, HALF)] = last
        send(g_send, g_recv, ds_sem, dr_sem, z_peer, j).wait_recv()
        wait_chunk(mb, m_sem, j)
        wait_chunk(vb, v_sem, j)

        def slab(i, carry):
            rows = pl.ds(pl.multiple_of(i * SLAB, SLAB), SLAB)
            gr = grad[rows, :] + g_recv[j, rows, :].astype(F32)
            first_new = 0.9 * mb[j, rows, :] + 0.1 * gr
            second_new = 0.95 * vb[j, rows, :] + 0.05 * gr * gr
            mb[j, rows, :] = first_new
            vb[j, rows, :] = second_new
            weights = pb[j, rows, :]
            update = first_new * scale_first / (jnp.sqrt(second_new * scale_second) + 1e-08)
            updated = weights - 0.01 * (update + 0.1 * weights)
            pb[j, rows, :] = updated
            u_send[j, rows, :] = updated.astype(BF16)
            return carry

        lax.fori_loop(0, pair // SLAB, slab, 0)

    def average(j):
        send(u_send, u_recv, us_sem, ur_sem, after, j).wait_recv()
        pb[j] = 0.5 * (pb[j] + u_recv[j].astype(F32))
        store(np_ref, pb, po_sem, j)

    def input_gradient(j):
        send(ig_send, ig_recv, is_sem, ir_sem, twin, j).wait_recv()
        ig_out[j] = (back_project(mine, j) + ig_recv[j]).astype(BF16)
        pltpu.make_async_copy(ig_out.at[j], ig_ref.at[:, cols(j)], io_sem.at[j]).start()

    def update_step(j):
        adam(j)
        send(u_send, u_recv, us_sem, ur_sem, after, j).start()
        store(nm_ref, mb, mo_sem, j)
        store(nv_ref, vb, vo_sem, j)
        ig_send[j] = back_project(other, j)
        send(ig_send, ig_recv, is_sem, ir_sem, twin, j).start()

        @pl.when(j >= 1)
        def _():
            input_gradient(j - 1)

        @pl.when(j >= LAG)
        def _():
            average(j - LAG)

    loop(update_step)
    input_gradient(count - 1)
    for j in range(count - LAG, count):
        average(j)

    def drain(j):
        send(w_own, w_rem, ws_sem, wr_sem, z_peer, j).wait_send()
        tokens_over(x_ref, xb, xs_sem, xr_sem, j).wait_send()
        tokens_over(g_ref, gb, gs_sem, gr_sem, j).wait_send()
        send(g_send, g_recv, ds_sem, dr_sem, z_peer, j).wait_send()
        send(u_send, u_recv, us_sem, ur_sem, after, j).wait_send()
        send(ig_send, ig_recv, is_sem, ir_sem, twin, j).wait_send()
        wait_chunk(pb, po_sem, j)
        wait_chunk(mb, mo_sem, j)
        wait_chunk(vb, vo_sem, j)
        pltpu.make_async_copy(ig_out.at[j], ig_ref.at[:, cols(j)], io_sem.at[j]).wait()

    loop(drain)


def window(by, collective_id, scales, inputs, grad_out, params, first, second):
    tok, width = inputs.shape
    hid = params.shape[2]
    pair = 2 * hid
    count = width // CHUNK
    anywhere = pl.BlockSpec(memory_space=pl.ANY)
    block = pltpu.VMEM((count, pair, WIDE), BF16)
    wide = pltpu.VMEM((count, pair, WIDE), F32)
    token = pltpu.VMEM((count, 2 * tok, CHUNK), BF16)
    partial = pltpu.VMEM((count, tok, CHUNK), F32)
    like = jax.ShapeDtypeStruct(params.shape, F32)
    return pl.pallas_call(
        functools.partial(window_kernel, by),
        out_shape=[like, like, like, jax.ShapeDtypeStruct(inputs.shape, BF16)],
        in_specs=[pl.BlockSpec(memory_space=pltpu.SMEM)] + [anywhere] * 5,
        out_specs=[anywhere] * 4,
        scratch_shapes=[token] * 2 + [wide] * 3 + [block] * 6 + [partial] * 2
        + [pltpu.VMEM((count, tok, CHUNK), BF16)]
        + [pltpu.VMEM((pair, 2 * tok), F32), pltpu.VMEM((hid, 2 * tok), F32)]
        + [pltpu.VMEM((pair, WIDE), F32)]
        + [pltpu.VMEM((pair, 2 * tok), BF16)] * 2
        + [pltpu.VMEM((hid + 8, 2 * tok), BF16)] * 2
        + [pltpu.SemaphoreType.DMA((count,))] * 21,
        compiler_params=pltpu.CompilerParams(
            collective_id=collective_id, has_side_effects=True,
            vmem_limit_bytes=40 * 2 ** 20),
        name=f"window_by_{by}",
    )(scales, inputs, grad_out, params, first, second)


def copy_kernel(n, *refs):
    sources, targets, sem = refs[:n], refs[n: 2 * n], refs[2 * n]
    copies = []
    for source, target in zip(sources, targets):
        if len(source.shape) == 4:
            pieces = [(source.at[0, i], target.at[0, i]) for i in range(source.shape[1])]
        else:
            pieces = [(source, target)]
        for a, b in pieces:
            copies.append(pltpu.make_async_copy(a, b, sem.at[len(copies)]))
    for copy in copies:
        copy.start()
    for copy in copies:
        copy.wait()


def hand_over(arrays):
    n = len(arrays)
    anywhere = pl.BlockSpec(memory_space=pl.ANY)
    return pl.pallas_call(
        functools.partial(copy_kernel, n),
        out_shape=[jax.ShapeDtypeStruct(a.shape, a.dtype) for a in arrays],
        in_specs=[anywhere] * n,
        out_specs=[anywhere] * n,
        scratch_shapes=[pltpu.SemaphoreType.DMA((3 * n,))],
        compiler_params=pltpu.CompilerParams(vmem_limit_bytes=16 * 2 ** 20),
        name="hand_over",
    )(*arrays)


def make_branch(bit):

    def run(*values):
        return tuple(hand_over(window(1 << bit, bit, *values)))

    return run


def per_device(step_index, inputs, grad_out, params, first_moment, second_moment):
    bits = lax.axis_size("rep").bit_length() - 1
    count_now = (step_index[0] + 1).astype(F32)
    fixes = 1.0 - jnp.power(jnp.array([0.9, 0.95], F32), count_now)
    branches = [make_branch(bit) for bit in range(bits)]
    return lax.switch(
        step_index[0] % bits, branches, 1.0 / fixes,
        inputs, grad_out, params, first_moment, second_moment)


def solution(mesh):
    return jax.shard_map(
        per_device,
        mesh=mesh,
        in_specs=(
            P(),
            P(("rep", "tp"), None),
            P(("rep", "tp"), None),
            P("rep", None, "tp", None),
            P("rep", None, "tp", None),
            P("rep", None, "tp", None),
        ),
        out_specs=(
            P("rep", None, "tp", None),
            P("rep", None, "tp", None),
            P("rep", None, "tp", None),
            P(("rep", "tp"), None),
        ),
        check_vma=False,
    )
```

```python
import functools
import math
import jax
import jax.numpy as jnp
from jax import lax
from jax.experimental import pallas as pl
from jax.experimental.pallas import tpu as pltpu
from jax.sharding import PartitionSpec as P

CHUNK = 512
HALF = CHUNK // 2
WIDE = CHUNK + HALF
LAG = 2
MESH = pl.DeviceIdType.MESH
BF16 = jnp.bfloat16
F32 = jnp.float32
NT = (((1,), (1,)), ((), ()))
NN = (((1,), (0,)), ((), ()))
TN = (((0,), (0,)), ((), ()))


def dot(a, b, dims):
    return lax.dot_general(a, b, dims, preferred_element_type=F32)


def window_kernel(
    by, groups,
    step_ref, x_ref, g_ref, p_ref, m_ref, v_ref,
    np_ref, nm_ref, nv_ref, ig_ref,
    xb, gb, step, ig_send, ig_recv, grad, *rest,
):
    n_groups = len(groups)
    rest = list(rest)

    def take(n):
        out = rest[:n]
        del rest[:n]
        return out

    w_own, w_rem, g_send, g_recv, u_send, u_recv = [take(n_groups) for _ in range(6)]
    acc_a, acc_b, d_own, d_rem, h_own, h_rem = [take(n_groups) for _ in range(6)]
    p_sem, w_sem, d_sem, u_sem, ig_sem, once, ready = rest

    n_rep = lax.axis_size("rep")
    rep = lax.axis_index("rep")
    tp = lax.axis_index("tp")
    core = lax.rem(tp, 2)
    z_peer = (rep, lax.rem(tp + 2, 4))
    twin = (rep, tp + 1 - 2 * core)
    after = (lax.rem(rep + by, n_rep), tp)
    before = (lax.rem(rep + n_rep - by, n_rep), tp)

    tok, width = x_ref.shape
    count = width // CHUNK
    mine = pl.ds(pl.multiple_of(core * tok, tok), tok)
    other = pl.ds(pl.multiple_of((1 - core) * tok, tok), tok)
    wide = pl.ds(0, CHUNK)
    narrow = pl.ds(CHUNK, HALF)
    halves = (pl.ds(0, HALF), pl.ds(HALF, HALF))

    def cols(j):
        return pl.ds(pl.multiple_of(j * CHUNK, CHUNK), CHUNK)

    def half(j, side):
        return pl.ds(pl.multiple_of(j * CHUNK + side * HALF, HALF), HALF)

    def loop(body):
        def trip(j, carry):
            body(j)
            return carry
        lax.fori_loop(0, count, trip, 0)

    def load_rows(g, j):
        start, size = groups[g]
        rows = pl.ds(start, size)
        return pltpu.make_async_copy(
            p_ref.at[0, :, rows, cols(j)], np_ref.at[0, :, rows, cols(j)], p_sem.at[g, j])

    def local(i):
        a, b = [
            (x_ref, xb.at[mine, :]), (g_ref, gb.at[mine, :]),
            (m_ref, nm_ref), (v_ref, nv_ref), (step_ref, step)][i]
        return pltpu.make_async_copy(a, b, once.at[i])

    def tokens_over(i):
        a, b = [(x_ref, xb), (g_ref, gb)][i]
        return pltpu.make_async_remote_copy(
            src_ref=a, dst_ref=b.at[mine, :],
            send_sem=once.at[5 + i], recv_sem=once.at[7 + i],
            device_id=twin, device_id_type=MESH)

    def unit(src, dst, sem, device, g, j):
        return pltpu.make_async_remote_copy(
            src_ref=src[g].at[j], dst_ref=dst[g].at[j],
            send_sem=sem.at[g, count], recv_sem=sem.at[g, j],
            device_id=device, device_id_type=MESH)

    def all_sent(src, dst, sem, device, g):
        pltpu.make_async_remote_copy(
            src_ref=src[g], dst_ref=dst[g],
            send_sem=sem.at[g, count], recv_sem=sem.at[g, 0],
            device_id=device, device_id_type=MESH).wait_send()

    barrier = pltpu.get_barrier_semaphore()
    for device in (z_peer, twin, after):
        pl.semaphore_signal(barrier, inc=1, device_id=device, device_id_type=MESH)
    for g in range(n_groups):
        loop(lambda j: load_rows(g, j).start())
    local(0).start()
    local(1).start()
    local(4).start()
    pl.semaphore_wait(barrier, 3)

    def weights_over(g, j):
        start, size = groups[g]
        load_rows(g, j).wait()
        rows = pl.ds(start, size)
        gate_up = [np_ref[0, i, rows, cols(j)] for i in range(2)]
        down = [np_ref[0, 2, rows, half(j, side)] for side in range(2)]
        w_own[g][j, :, wide] = jnp.concatenate(gate_up, axis=0).astype(BF16)
        w_own[g][j, :, narrow] = jnp.concatenate(down, axis=0).astype(BF16)
        unit(w_own, w_rem, w_sem, z_peer, g, j).start()

    for g in range(n_groups):
        loop(functools.partial(weights_over, g))
        if g == 0:
            tokens_over(0).start()
            tokens_over(1).start()
    pl.semaphore_signal(ready, inc=1, device_id=before, device_id_type=MESH)
    local(2).start()
    local(3).start()

    def project(w, g, j):
        size = groups[g][1]
        low = size // 16 * 16
        high = 2 * size - low
        acc_a[g][...] += dot(w[g][j, :, wide], xb[:, cols(j)], NT)
        left = dot(w[g][j, pl.ds(0, high), narrow], gb[:, half(j, 0)], NT)
        right = dot(w[g][j, pl.ds(low, high), narrow], gb[:, half(j, 1)], NT)
        acc_b[g][...] += left[:size] + right[size - low:]

    def start_sums(g):
        acc_a[g][...] = jnp.zeros_like(acc_a[g])
        acc_b[g][...] = jnp.zeros_like(acc_b[g])

    def finish_hidden(d_ref, h_ref, g):
        size = groups[g][1]
        pre_gate = acc_a[g][pl.ds(0, size), :]
        pre_up = acc_a[g][pl.ds(size, size), :]
        back = acc_b[g][...]
        s = jax.nn.sigmoid(pre_gate)
        silu = s * pre_gate
        hidden = silu * pre_up
        more = h_ref[g].shape[0] - size
        if more:
            hidden = jnp.concatenate([hidden, jnp.zeros((more, 2 * tok), F32)], axis=0)
        h_ref[g][...] = hidden.astype(BF16)
        d_gate = back * pre_up * s * (1.0 + pre_gate * (1.0 - s))
        d_ref[g][...] = jnp.concatenate([d_gate, back * silu], axis=0).astype(BF16)

    local(0).wait()
    local(1).wait()
    tokens_over(0).wait_recv()
    tokens_over(1).wait_recv()
    for g in range(n_groups):
        start_sums(g)
        loop(functools.partial(project, w_own, g))
        finish_hidden(d_own, h_own, g)

    def project_rem(g, j):
        unit(w_own, w_rem, w_sem, z_peer, g, j).wait_recv()
        project(w_rem, g, j)

    def gradient(d_ref, h_ref, g, j):
        size = groups[g][1]
        first = dot(d_ref[g][...], xb[:, cols(j)], NN)
        last = dot(h_ref[g][...], gb[:, cols(j)], NN)[:size]
        return first, jnp.concatenate([last[:, :HALF], last[:, HALF:]], axis=0)

    def gradients_over(g, j):
        first, last = gradient(d_rem, h_rem, g, j)
        g_send[g][j, :, wide] = first.astype(BF16)
        g_send[g][j, :, narrow] = last.astype(BF16)
        unit(g_send, g_recv, d_sem, z_peer, g, j).start()

    for g in range(n_groups):
        start_sums(g)
        loop(functools.partial(project_rem, g))
        finish_hidden(d_rem, h_rem, g)
        if g < n_groups - 1:
            loop(functools.partial(gradients_over, g))

    local(4).wait()
    local(2).wait()
    local(3).wait()
    n = jnp.full((8, 128), step[0] + 1, jnp.int32).astype(F32)
    scale_first = (1.0 / (1.0 - jnp.exp(n * math.log(0.9))))[0, 0]
    scale_second = (1.0 / (1.0 - jnp.exp(n * math.log(0.95))))[0, 0]

    def pieces(g, j):
        start, size = groups[g]
        for q in range(0, 2 * size, 8):
            side, r = divmod(q, size)
            rows = pl.ds(start + r, 8)
            yield q, ((0, side, rows, cols(j)), (0, 2, rows, half(j, side)))

    def adam(g, j):
        size = groups[g][1]
        first, last = gradient(d_own, h_own, g, j)
        grad[pl.ds(0, 2 * size), wide] = first
        grad[pl.ds(0, 2 * size), narrow] = last
        unit(g_send, g_recv, d_sem, z_peer, g, j).wait_recv()
        spans = (wide, narrow)
        held = {}
        for q, places in pieces(g, j):
            for span, place in zip(spans, places):
                i = 0 if span is wide else 1
                rows = pl.ds(q // 16 * 16, 16)
                if q % 16 == 0:
                    held[i] = g_recv[g][j, rows, span].astype(F32)
                theirs = held[i][q % 16: q % 16 + 8]
                gr = grad[pl.ds(q, 8), span] + theirs
                first_new = 0.9 * nm_ref[place] + 0.1 * gr
                second_new = 0.95 * nv_ref[place] + 0.05 * gr * gr
                nm_ref[place] = first_new
                nv_ref[place] = second_new
                weights = np_ref[place]
                update = first_new * scale_first / (jnp.sqrt(second_new * scale_second) + 1e-08)
                updated = weights - 0.01 * (update + 0.1 * weights)
                np_ref[place] = updated
                if q % 16 == 0:
                    held[2 + i] = updated
                else:
                    both = jnp.concatenate([held[2 + i], updated], axis=0)
                    u_send[g][j, rows, span] = both.astype(BF16)
        unit(u_send, u_recv, u_sem, after, g, j).start()

    def average(g, j):
        unit(u_send, u_recv, u_sem, after, g, j).wait_recv()
        held = {}
        for q, places in pieces(g, j):
            for i, place in enumerate(places):
                if q % 16 == 0:
                    span = (wide, narrow)[i]
                    held[i] = u_recv[g][j, pl.ds(q, 16), span].astype(F32)
                np_ref[place] = 0.5 * (np_ref[place] + held[i][q % 16: q % 16 + 8])

    def back_project(rows, j):
        total = None
        for g in range(n_groups):
            for d_ref, w in ((d_own, w_own), (d_rem, w_rem)):
                term = dot(d_ref[g][:, rows], w[g][j, :, wide], TN)
                total = term if total is None else total + term
        return total

    def input_over(j):
        return pltpu.make_async_remote_copy(
            src_ref=ig_send.at[j], dst_ref=ig_recv.at[j],
            send_sem=ig_sem.at[count], recv_sem=ig_sem.at[j],
            device_id=twin, device_id_type=MESH)

    pl.semaphore_wait(ready, 1)
    last = n_groups - 1

    def first_pass(j):
        adam(0, j)
        gradients_over(last, j)
        ig_send[j] = back_project(other, j)
        input_over(j).start()

    def last_pass(j):
        adam(last, j)
        average(0, j)
        input_over(j).wait_recv()
        ig_ref[:, cols(j)] = (back_project(mine, j) + ig_recv[j]).astype(BF16)

        @pl.when(j >= LAG)
        def _():
            average(last, j - LAG)

    loop(first_pass)
    loop(last_pass)
    for g in range(n_groups):
        all_sent(w_own, w_rem, w_sem, z_peer, g)
        all_sent(g_send, g_recv, d_sem, z_peer, g)
    tokens_over(0).wait_send()
    tokens_over(1).wait_send()
    pltpu.make_async_remote_copy(
        src_ref=ig_send, dst_ref=ig_recv, send_sem=ig_sem.at[count], recv_sem=ig_sem.at[0],
        device_id=twin, device_id_type=MESH).wait_send()
    for j in range(count - LAG, count):
        average(last, j)
    for g in range(n_groups):
        all_sent(u_send, u_recv, u_sem, after, g)


def window(by, collective_id, step_index, inputs, grad_out, params, first, second):
    tok, width = inputs.shape
    hid = params.shape[2]
    count = width // CHUNK
    split = hid // 16 * 8
    groups = ((0, split), (split, hid - split))
    anywhere = pl.BlockSpec(memory_space=pl.ANY)
    inside = pl.BlockSpec(memory_space=pltpu.VMEM)
    like = jax.ShapeDtypeStruct(params.shape, F32)

    def each(make):
        return [make(size) for _, size in groups]

    blocks = each(lambda n: pltpu.VMEM((count, 2 * n, WIDE), BF16))
    sums = each(lambda n: pltpu.VMEM((2 * n, 2 * tok), F32)) + each(
        lambda n: pltpu.VMEM((n, 2 * tok), F32))
    d_refs = each(lambda n: pltpu.VMEM((2 * n, 2 * tok), BF16))
    h_refs = each(lambda n: pltpu.VMEM((-(-n // 16) * 16, 2 * tok), BF16))
    units = pltpu.SemaphoreType.DMA((len(groups), count + 1))
    return pl.pallas_call(
        functools.partial(window_kernel, by, groups),
        out_shape=[like, like, like, jax.ShapeDtypeStruct(inputs.shape, BF16)],
        in_specs=[anywhere] * 6,
        out_specs=[inside] * 4,
        scratch_shapes=[pltpu.VMEM((2 * tok, width), BF16)] * 2
        + [pltpu.SMEM((1,), jnp.int32)]
        + [pltpu.VMEM((count, tok, CHUNK), F32)] * 2
        + [pltpu.VMEM((2 * hid, WIDE), F32)]
        + blocks * 6 + sums + d_refs * 2 + h_refs * 2
        + [units] * 4
        + [pltpu.SemaphoreType.DMA((count + 1,)), pltpu.SemaphoreType.DMA((9,)),
           pltpu.SemaphoreType.REGULAR],
        compiler_params=pltpu.CompilerParams(
            collective_id=collective_id, has_side_effects=True,
            vmem_limit_bytes=40 * 2 ** 20),
        name=f"window_by_{by}",
    )(step_index, inputs, grad_out, params, first, second)


def copy_kernel(n, *refs):
    sources, targets, sem = refs[:n], refs[n: 2 * n], refs[2 * n]
    copies = []
    for source, target in zip(sources, targets):
        if len(source.shape) == 4:
            pieces = [(source.at[0, i], target.at[0, i]) for i in range(source.shape[1])]
        else:
            pieces = [(source, target)]
        for a, b in pieces:
            copies.append(pltpu.make_async_copy(a, b, sem.at[len(copies)]))
    for copy in copies:
        copy.start()
    for copy in copies:
        copy.wait()


def hand_over(arrays):
    n = len(arrays)
    anywhere = pl.BlockSpec(memory_space=pl.ANY)
    return pl.pallas_call(
        functools.partial(copy_kernel, n),
        out_shape=[jax.ShapeDtypeStruct(a.shape, a.dtype) for a in arrays],
        in_specs=[anywhere] * n,
        out_specs=[anywhere] * n,
        scratch_shapes=[pltpu.SemaphoreType.DMA((3 * n,))],
        compiler_params=pltpu.CompilerParams(vmem_limit_bytes=16 * 2 ** 20),
        name="hand_over",
    )(*arrays)


def make_branch(bit):

    def run(*values):
        return tuple(hand_over(window(1 << bit, bit, *values)))

    return run


def per_device(step_index, inputs, grad_out, params, first_moment, second_moment):
    bits = lax.axis_size("rep").bit_length() - 1
    branches = [make_branch(bit) for bit in range(bits)]
    return lax.switch(
        step_index[0] % bits, branches,
        step_index, inputs, grad_out, params, first_moment, second_moment)


def solution(mesh):
    return jax.shard_map(
        per_device,
        mesh=mesh,
        in_specs=(
            P(),
            P(("rep", "tp"), None),
            P(("rep", "tp"), None),
            P("rep", None, "tp", None),
            P("rep", None, "tp", None),
            P("rep", None, "tp", None),
        ),
        out_specs=(
            P("rep", None, "tp", None),
            P("rep", None, "tp", None),
            P("rep", None, "tp", None),
            P(("rep", "tp"), None),
        ),
        check_vma=False,
    )
```

```python
import functools
import math
import jax
import jax.numpy as jnp
from jax import lax
from jax.experimental import pallas as pl
from jax.experimental.pallas import tpu as pltpu
from jax.sharding import PartitionSpec as P

CHUNK = 512
HALF = CHUNK // 2
WIDE = CHUNK + HALF
LAG = 2
MESH = pl.DeviceIdType.MESH
BF16 = jnp.bfloat16
F32 = jnp.float32
NT = (((1,), (1,)), ((), ()))
NN = (((1,), (0,)), ((), ()))
TN = (((0,), (0,)), ((), ()))


def dot(a, b, dims):
    return lax.dot_general(a, b, dims, preferred_element_type=F32)


def window_kernel(
    by, groups,
    step_ref, x_ref, g_ref, p_ref, m_ref, v_ref,
    np_ref, nm_ref, nv_ref, ig_ref,
    xb, gb, step, ig_send, ig_recv, grad, *rest,
):
    n_groups = len(groups)
    rest = list(rest)

    def take(n):
        out = rest[:n]
        del rest[:n]
        return out

    w_own, w_rem, g_send, g_recv, u_send, u_recv = [take(n_groups) for _ in range(6)]
    acc_a, acc_b, d_own, d_rem, h_own, h_rem = [take(n_groups) for _ in range(6)]
    p_sem, w_sem, d_sem, u_sem, ig_sem, once = rest

    n_rep = lax.axis_size("rep")
    rep = lax.axis_index("rep")
    tp = lax.axis_index("tp")
    core = lax.rem(tp, 2)
    z_peer = (rep, lax.rem(tp + 2, 4))
    twin = (rep, tp + 1 - 2 * core)
    after = (lax.rem(rep + by, n_rep), tp)
    before = (lax.rem(rep + n_rep - by, n_rep), tp)

    tok, width = x_ref.shape
    count = width // CHUNK
    mine = pl.ds(pl.multiple_of(core * tok, tok), tok)
    other = pl.ds(pl.multiple_of((1 - core) * tok, tok), tok)
    wide = pl.ds(0, CHUNK)
    narrow = pl.ds(CHUNK, HALF)
    halves = (pl.ds(0, HALF), pl.ds(HALF, HALF))

    def cols(j):
        return pl.ds(pl.multiple_of(j * CHUNK, CHUNK), CHUNK)

    def half(j, side):
        return pl.ds(pl.multiple_of(j * CHUNK + side * HALF, HALF), HALF)

    def loop(body, low=0, high=count):
        def trip(j, carry):
            body(j)
            return carry
        lax.fori_loop(low, high, trip, 0)

    def load_rows(g, j):
        start, size = groups[g]
        rows = pl.ds(start, size)
        return pltpu.make_async_copy(
            p_ref.at[0, :, rows, cols(j)], np_ref.at[0, :, rows, cols(j)], p_sem.at[g, j])

    def local(i):
        a, b = [
            (x_ref, xb.at[mine, :]), (g_ref, gb.at[mine, :]),
            (m_ref, nm_ref), (v_ref, nv_ref), (step_ref, step)][i]
        return pltpu.make_async_copy(a, b, once.at[i])

    def tokens_over(i):
        a, b = [(x_ref, xb), (g_ref, gb)][i]
        return pltpu.make_async_remote_copy(
            src_ref=a, dst_ref=b.at[mine, :],
            send_sem=once.at[5 + i], recv_sem=once.at[7 + i],
            device_id=twin, device_id_type=MESH)

    def unit(src, dst, sem, device, g, j):
        return pltpu.make_async_remote_copy(
            src_ref=src[g].at[j], dst_ref=dst[g].at[j],
            send_sem=sem.at[g, count], recv_sem=sem.at[g, j],
            device_id=device, device_id_type=MESH)

    parts = ((0, count // 2), (count // 2, count - 2), (count - 2, count))

    def weights(g, low, high):
        span = pl.ds(low, 1 if high is None else high - low)
        return pltpu.make_async_remote_copy(
            src_ref=w_own[g].at[span], dst_ref=w_rem[g].at[span],
            send_sem=w_sem.at[g, count], recv_sem=w_sem.at[g, low],
            device_id=z_peer, device_id_type=MESH)

    def all_sent(src, dst, sem, device, g):
        pltpu.make_async_remote_copy(
            src_ref=src[g], dst_ref=dst[g],
            send_sem=sem.at[g, count], recv_sem=sem.at[g, 0],
            device_id=device, device_id_type=MESH).wait_send()

    barrier = pltpu.get_barrier_semaphore()
    load_rows(0, 0).start()
    for device in (z_peer, twin, before):
        pl.semaphore_signal(barrier, inc=1, device_id=device, device_id_type=MESH)
    for g in range(n_groups):
        loop(lambda j: load_rows(g, j).start(), 1 - min(g, 1))
    pl.semaphore_wait(barrier, 3)

    def weights_over(g, j):
        start, size = groups[g]
        load_rows(g, j).wait()
        rows = pl.ds(start, size)
        gate_up = [np_ref[0, i, rows, cols(j)] for i in range(2)]
        down = [np_ref[0, 2, rows, half(j, side)] for side in range(2)]
        w_own[g][j, :, wide] = jnp.concatenate(gate_up, axis=0).astype(BF16)
        w_own[g][j, :, narrow] = jnp.concatenate(down, axis=0).astype(BF16)
        if g == 0:
            weights(0, j, None).start()

    for g in range(n_groups):
        loop(functools.partial(weights_over, g))
        if g == 0:
            for i in range(2):
                local(i).start()
                tokens_over(i).start()
            local(4).start()
        else:
            for low, high in parts:
                weights(g, low, high).start()
    local(2).start()
    local(3).start()

    def project(w, g, j):
        size = groups[g][1]
        low = size // 16 * 16
        high = 2 * size - low
        acc_a[g][...] += dot(w[g][j, :, wide], xb[:, cols(j)], NT)
        left = dot(w[g][j, pl.ds(0, high), narrow], gb[:, half(j, 0)], NT)
        right = dot(w[g][j, pl.ds(low, high), narrow], gb[:, half(j, 1)], NT)
        acc_b[g][...] += left[:size] + right[size - low:]

    def start_sums(g):
        acc_a[g][...] = jnp.zeros_like(acc_a[g])
        acc_b[g][...] = jnp.zeros_like(acc_b[g])

    def finish_hidden(d_ref, h_ref, g):
        size = groups[g][1]
        pre_gate = acc_a[g][pl.ds(0, size), :]
        pre_up = acc_a[g][pl.ds(size, size), :]
        back = acc_b[g][...]
        small = jnp.exp(-jnp.abs(pre_gate))
        s = jnp.where(pre_gate >= 0.0, 1.0, small) / (1.0 + small)
        silu = s * pre_gate
        hidden = silu * pre_up
        more = h_ref[g].shape[0] - size
        if more:
            hidden = jnp.concatenate([hidden, jnp.zeros((more, 2 * tok), F32)], axis=0)
        h_ref[g][...] = hidden.astype(BF16)
        d_gate = back * pre_up * s * (1.0 + pre_gate * (1.0 - s))
        d_ref[g][...] = jnp.concatenate([d_gate, back * silu], axis=0).astype(BF16)

    local(0).wait()
    local(1).wait()
    tokens_over(0).wait_recv()
    tokens_over(1).wait_recv()
    for g in range(n_groups):
        start_sums(g)
        loop(functools.partial(project, w_own, g))
        finish_hidden(d_own, h_own, g)

    def project_rem(j):
        weights(0, j, None).wait_recv()
        project(w_rem, 0, j)

    def gradient(d_ref, h_ref, g, j):
        size = groups[g][1]
        first = dot(d_ref[g][...], xb[:, cols(j)], NN)
        last = dot(h_ref[g][...], gb[:, cols(j)], NN)[:size]
        return first, jnp.concatenate([last[:, :HALF], last[:, HALF:]], axis=0)

    def gradients_over(g, j):
        first, last = gradient(d_rem, h_rem, g, j)
        g_send[g][j, :, wide] = first.astype(BF16)
        g_send[g][j, :, narrow] = last.astype(BF16)
        unit(g_send, g_recv, d_sem, z_peer, g, j).start()

    for g in range(n_groups):
        start_sums(g)
        if g == 0:
            loop(project_rem)
        else:
            for low, high in parts:
                weights(g, low, high).wait_recv()
                loop(functools.partial(project, w_rem, g), low, high)
        finish_hidden(d_rem, h_rem, g)
        if g < n_groups - 1:
            loop(functools.partial(gradients_over, g))

    local(4).wait()
    local(2).wait()
    local(3).wait()
    n = jnp.full((8, 128), step[0] + 1, jnp.int32).astype(F32)
    scale_first = (1.0 / (1.0 - jnp.exp(n * math.log(0.9))))[0, 0]
    scale_second = (1.0 / (1.0 - jnp.exp(n * math.log(0.95))))[0, 0]

    def pieces(g, j):
        start, size = groups[g]
        for q in range(0, 2 * size, 8):
            side, r = divmod(q, size)
            rows = pl.ds(start + r, 8)
            yield q, ((0, side, rows, cols(j)), (0, 2, rows, half(j, side)))

    def adam(g, j):
        size = groups[g][1]
        first, last = gradient(d_own, h_own, g, j)
        grad[pl.ds(0, 2 * size), wide] = first
        grad[pl.ds(0, 2 * size), narrow] = last
        unit(g_send, g_recv, d_sem, z_peer, g, j).wait_recv()
        spans = (wide, narrow)
        held = {}
        for q, places in pieces(g, j):
            for span, place in zip(spans, places):
                i = 0 if span is wide else 1
                rows = pl.ds(q // 16 * 16, 16)
                if q % 16 == 0:
                    held[i] = g_recv[g][j, rows, span].astype(F32)
                theirs = held[i][q % 16: q % 16 + 8]
                gr = grad[pl.ds(q, 8), span] + theirs
                first_new = 0.9 * nm_ref[place] + 0.1 * gr
                second_new = 0.95 * nv_ref[place] + 0.05 * gr * gr
                nm_ref[place] = first_new
                nv_ref[place] = second_new
                weights = np_ref[place]
                update = first_new * scale_first / (jnp.sqrt(second_new * scale_second) + 1e-08)
                updated = weights - 0.01 * (update + 0.1 * weights)
                np_ref[place] = updated
                if q % 16 == 0:
                    held[2 + i] = updated
                else:
                    both = jnp.concatenate([held[2 + i], updated], axis=0)
                    u_send[g][j, rows, span] = both.astype(BF16)
        unit(u_send, u_recv, u_sem, after, g, j).start()

    def average(g, j):
        unit(u_send, u_recv, u_sem, after, g, j).wait_recv()
        held = {}
        for q, places in pieces(g, j):
            for i, place in enumerate(places):
                if q % 16 == 0:
                    span = (wide, narrow)[i]
                    held[i] = u_recv[g][j, pl.ds(q, 16), span].astype(F32)
                np_ref[place] = 0.5 * (np_ref[place] + held[i][q % 16: q % 16 + 8])

    def back_project(rows, j):
        total = None
        for g in range(n_groups):
            for d_ref, w in ((d_own, w_own), (d_rem, w_rem)):
                term = dot(d_ref[g][:, rows], w[g][j, :, wide], TN)
                total = term if total is None else total + term
        return total

    def input_over(j):
        return pltpu.make_async_remote_copy(
            src_ref=ig_send.at[j], dst_ref=ig_recv.at[j],
            send_sem=ig_sem.at[count], recv_sem=ig_sem.at[j],
            device_id=twin, device_id_type=MESH)

    last = n_groups - 1

    def first_pass(j):
        adam(0, j)
        gradients_over(last, j)
        ig_send[j] = back_project(other, j)
        input_over(j).start()

    def last_pass(j):
        adam(last, j)
        average(0, j)
        input_over(j).wait_recv()
        ig_ref[:, cols(j)] = (back_project(mine, j) + ig_recv[j]).astype(BF16)

        @pl.when(j >= LAG)
        def _():
            average(last, j - LAG)

    loop(first_pass)
    loop(last_pass)
    for g in range(n_groups):
        all_sent(w_own, w_rem, w_sem, z_peer, g)
        all_sent(g_send, g_recv, d_sem, z_peer, g)
    tokens_over(0).wait_send()
    tokens_over(1).wait_send()
    pltpu.make_async_remote_copy(
        src_ref=ig_send, dst_ref=ig_recv, send_sem=ig_sem.at[count], recv_sem=ig_sem.at[0],
        device_id=twin, device_id_type=MESH).wait_send()
    for j in range(count - LAG, count):
        average(last, j)
    for g in range(n_groups):
        all_sent(u_send, u_recv, u_sem, after, g)


def window(by, collective_id, step_index, inputs, grad_out, params, first, second):
    tok, width = inputs.shape
    hid = params.shape[2]
    count = width // CHUNK
    split = hid // 16 * 8
    groups = ((0, split), (split, hid - split))
    anywhere = pl.BlockSpec(memory_space=pl.ANY)
    inside = pl.BlockSpec(memory_space=pltpu.VMEM)
    like = jax.ShapeDtypeStruct(params.shape, F32)

    def each(make):
        return [make(size) for _, size in groups]

    blocks = each(lambda n: pltpu.VMEM((count, 2 * n, WIDE), BF16))
    sums = each(lambda n: pltpu.VMEM((2 * n, 2 * tok), F32)) + each(
        lambda n: pltpu.VMEM((n, 2 * tok), F32))
    d_refs = each(lambda n: pltpu.VMEM((2 * n, 2 * tok), BF16))
    h_refs = each(lambda n: pltpu.VMEM((-(-n // 16) * 16, 2 * tok), BF16))
    units = pltpu.SemaphoreType.DMA((len(groups), count + 1))
    return pl.pallas_call(
        functools.partial(window_kernel, by, groups),
        out_shape=[like, like, like, jax.ShapeDtypeStruct(inputs.shape, BF16)],
        in_specs=[anywhere] * 6,
        out_specs=[inside] * 4,
        scratch_shapes=[pltpu.VMEM((2 * tok, width), BF16)] * 2
        + [pltpu.SMEM((1,), jnp.int32)]
        + [pltpu.VMEM((count, tok, CHUNK), F32)] * 2
        + [pltpu.VMEM((2 * hid, WIDE), F32)]
        + blocks * 6 + sums + d_refs * 2 + h_refs * 2
        + [units] * 4
        + [pltpu.SemaphoreType.DMA((count + 1,)), pltpu.SemaphoreType.DMA((9,))],
        compiler_params=pltpu.CompilerParams(
            collective_id=collective_id, has_side_effects=True,
            vmem_limit_bytes=40 * 2 ** 20),
        name=f"window_by_{by}",
    )(step_index, inputs, grad_out, params, first, second)


def copy_kernel(n, *refs):
    sources, targets, sem = refs[:n], refs[n: 2 * n], refs[2 * n]
    copies = []
    for source, target in zip(sources, targets):
        if len(source.shape) == 4:
            pieces = [(source.at[0, i], target.at[0, i]) for i in range(source.shape[1])]
        else:
            pieces = [(source, target)]
        for a, b in pieces:
            copies.append(pltpu.make_async_copy(a, b, sem.at[len(copies)]))
    for copy in copies:
        copy.start()
    for copy in copies:
        copy.wait()


def hand_over(arrays):
    n = len(arrays)
    anywhere = pl.BlockSpec(memory_space=pl.ANY)
    return pl.pallas_call(
        functools.partial(copy_kernel, n),
        out_shape=[jax.ShapeDtypeStruct(a.shape, a.dtype) for a in arrays],
        in_specs=[anywhere] * n,
        out_specs=[anywhere] * n,
        scratch_shapes=[pltpu.SemaphoreType.DMA((3 * n,))],
        compiler_params=pltpu.CompilerParams(vmem_limit_bytes=16 * 2 ** 20),
        name="hand_over",
    )(*arrays)


def make_branch(bit):

    def run(*values):
        return tuple(hand_over(window(1 << bit, bit, *values)))

    return run


def per_device(step_index, inputs, grad_out, params, first_moment, second_moment):
    bits = lax.axis_size("rep").bit_length() - 1
    branches = [make_branch(bit) for bit in range(bits)]
    return lax.switch(
        step_index[0] % bits, branches,
        step_index, inputs, grad_out, params, first_moment, second_moment)


def solution(mesh):
    return jax.shard_map(
        per_device,
        mesh=mesh,
        in_specs=(
            P(),
            P(("rep", "tp"), None),
            P(("rep", "tp"), None),
            P("rep", None, "tp", None),
            P("rep", None, "tp", None),
            P("rep", None, "tp", None),
        ),
        out_specs=(
            P("rep", None, "tp", None),
            P("rep", None, "tp", None),
            P("rep", None, "tp", None),
            P(("rep", "tp"), None),
        ),
        check_vma=False,
    )
```

```python
import functools
import math
import jax
import jax.numpy as jnp
from jax import lax
from jax.experimental import pallas as pl
from jax.experimental.pallas import tpu as pltpu
from jax.sharding import PartitionSpec as P

SEND = 512
MESH = pl.DeviceIdType.MESH
BF16 = jnp.bfloat16
F32 = jnp.float32
NT = (((1,), (1,)), ((), ()))
NN = (((1,), (0,)), ((), ()))
TN = (((0,), (0,)), ((), ()))


def dot(a, b, dims):
    return lax.dot_general(a, b, dims, preferred_element_type=F32)


def window_kernel(
    by, groups, chunk,
    step_ref, x_ref, g_ref, p_ref, m_ref, v_ref,
    np_ref, nm_ref, nv_ref, ig_ref,
    xb, gb, step, ig_send, ig_recv, grad, *rest,
):
    n_groups = len(groups)
    half_chunk = chunk // 2
    per_send = SEND // chunk
    lag = 2 * per_send
    rest = list(rest)

    def take(n):
        out = rest[:n]
        del rest[:n]
        return out

    w_own, w_rem, g_send, g_recv, u_send, u_recv = [take(n_groups) for _ in range(6)]
    acc_a, acc_b, d_own, d_rem, h_own, h_rem = [take(n_groups) for _ in range(6)]
    p_sem, w_sem, d_sem, u_sem, ig_sem, once = rest

    n_rep = lax.axis_size("rep")
    rep = lax.axis_index("rep")
    tp = lax.axis_index("tp")
    core = lax.rem(tp, 2)
    z_peer = (rep, lax.rem(tp + 2, 4))
    twin = (rep, tp + 1 - 2 * core)
    after = (lax.rem(rep + by, n_rep), tp)
    before = (lax.rem(rep + n_rep - by, n_rep), tp)

    tok, width = x_ref.shape
    count = width // chunk
    mine = pl.ds(pl.multiple_of(core * tok, tok), tok)
    other = pl.ds(pl.multiple_of((1 - core) * tok, tok), tok)
    wide = pl.ds(0, chunk)
    narrow = pl.ds(chunk, half_chunk)
    halves = (pl.ds(0, half_chunk), pl.ds(half_chunk, half_chunk))

    def cols(j):
        return pl.ds(pl.multiple_of(j * chunk, chunk), chunk)

    def half(j, side):
        return pl.ds(pl.multiple_of(j * chunk + side * half_chunk, half_chunk), half_chunk)

    def loop(body, low=0, high=count):
        def trip(j, carry):
            body(j)
            return carry
        lax.fori_loop(low, high, trip, 0)

    def load_rows(g, j):
        start, size = groups[g]
        rows = pl.ds(start, size)
        return pltpu.make_async_copy(
            p_ref.at[0, :, rows, cols(j)], np_ref.at[0, :, rows, cols(j)], p_sem.at[g, j])

    def local(i):
        a, b = [
            (x_ref, xb.at[mine, :]), (g_ref, gb.at[mine, :]),
            (m_ref, nm_ref), (v_ref, nv_ref), (step_ref, step)][i]
        return pltpu.make_async_copy(a, b, once.at[i])

    def tokens_over(i):
        a, b = [(x_ref, xb), (g_ref, gb)][i]
        return pltpu.make_async_remote_copy(
            src_ref=a, dst_ref=b.at[mine, :],
            send_sem=once.at[5 + i], recv_sem=once.at[7 + i],
            device_id=twin, device_id_type=MESH)

    def unit(src, dst, sem, device, g, j):
        return pltpu.make_async_remote_copy(
            src_ref=src[g].at[j], dst_ref=dst[g].at[j],
            send_sem=sem.at[g, count], recv_sem=sem.at[g, j],
            device_id=device, device_id_type=MESH)

    parts = ((0, count // 2), (count // 2, count - 2), (count - 2, count))

    def weights(g, low, n):
        span = pl.ds(low, n)
        return pltpu.make_async_remote_copy(
            src_ref=w_own[g].at[span], dst_ref=w_rem[g].at[span],
            send_sem=w_sem.at[g, count], recv_sem=w_sem.at[g, low],
            device_id=z_peer, device_id_type=MESH)

    def all_sent(src, dst, sem, device, g):
        pltpu.make_async_remote_copy(
            src_ref=src[g], dst_ref=dst[g],
            send_sem=sem.at[g, count], recv_sem=sem.at[g, 0],
            device_id=device, device_id_type=MESH).wait_send()

    barrier = pltpu.get_barrier_semaphore()
    load_rows(0, 0).start()
    for device in (z_peer, twin, before):
        pl.semaphore_signal(barrier, inc=1, device_id=device, device_id_type=MESH)
    for g in range(n_groups):
        loop(lambda j: load_rows(g, j).start(), 1 - min(g, 1))
    pl.semaphore_wait(barrier, 3)

    def weights_over(g, j):
        start, size = groups[g]
        load_rows(g, j).wait()
        rows = pl.ds(start, size)
        gate_up = [np_ref[0, i, rows, cols(j)] for i in range(2)]
        down = [np_ref[0, 2, rows, half(j, side)] for side in range(2)]
        w_own[g][j, :, wide] = jnp.concatenate(gate_up, axis=0).astype(BF16)
        w_own[g][j, :, narrow] = jnp.concatenate(down, axis=0).astype(BF16)
        if g == 0:
            @pl.when(lax.rem(j, per_send) == per_send - 1)
            def _():
                weights(0, j - (per_send - 1), per_send).start()

    for g in range(n_groups):
        loop(functools.partial(weights_over, g))
        if g == 0:
            for i in range(2):
                local(i).start()
                tokens_over(i).start()
            local(4).start()
        else:
            for low, high in parts:
                weights(g, low, high - low).start()
    local(2).start()
    local(3).start()

    def project(w, g, j):
        size = groups[g][1]
        low = size // 16 * 16
        high = 2 * size - low
        acc_a[g][...] += dot(w[g][j, :, wide], xb[:, cols(j)], NT)
        left = dot(w[g][j, pl.ds(0, high), narrow], gb[:, half(j, 0)], NT)
        right = dot(w[g][j, pl.ds(low, high), narrow], gb[:, half(j, 1)], NT)
        acc_b[g][...] += left[:size] + right[size - low:]

    def start_sums(g):
        acc_a[g][...] = jnp.zeros_like(acc_a[g])
        acc_b[g][...] = jnp.zeros_like(acc_b[g])

    def finish_hidden(d_ref, h_ref, g):
        size = groups[g][1]
        pre_gate = acc_a[g][pl.ds(0, size), :]
        pre_up = acc_a[g][pl.ds(size, size), :]
        back = acc_b[g][...]
        small = jnp.exp(-jnp.abs(pre_gate))
        s = jnp.where(pre_gate >= 0.0, 1.0, small) / (1.0 + small)
        silu = s * pre_gate
        hidden = silu * pre_up
        more = h_ref[g].shape[0] - size
        if more:
            hidden = jnp.concatenate([hidden, jnp.zeros((more, 2 * tok), F32)], axis=0)
        h_ref[g][...] = hidden.astype(BF16)
        d_gate = back * pre_up * s * (1.0 + pre_gate * (1.0 - s))
        d_ref[g][...] = jnp.concatenate([d_gate, back * silu], axis=0).astype(BF16)

    local(0).wait()
    local(1).wait()
    tokens_over(0).wait_recv()
    tokens_over(1).wait_recv()
    for g in range(n_groups):
        start_sums(g)
        loop(functools.partial(project, w_own, g))
        finish_hidden(d_own, h_own, g)

    def project_rem(j):
        @pl.when(lax.rem(j, per_send) == 0)
        def _():
            weights(0, j, per_send).wait_recv()

        project(w_rem, 0, j)

    def gradient(d_ref, h_ref, g, j):
        size = groups[g][1]
        first = dot(d_ref[g][...], xb[:, cols(j)], NN)
        last = dot(h_ref[g][...], gb[:, cols(j)], NN)[:size]
        return first, jnp.concatenate([last[:, :half_chunk], last[:, half_chunk:]], axis=0)

    def gradients_over(g, j):
        first, last = gradient(d_rem, h_rem, g, j)
        g_send[g][j, :, wide] = first.astype(BF16)
        g_send[g][j, :, narrow] = last.astype(BF16)
        unit(g_send, g_recv, d_sem, z_peer, g, j).start()

    for g in range(n_groups):
        start_sums(g)
        if g == 0:
            loop(project_rem)
        else:
            for low, high in parts:
                weights(g, low, high - low).wait_recv()
                loop(functools.partial(project, w_rem, g), low, high)
        finish_hidden(d_rem, h_rem, g)
        if g < n_groups - 1:
            loop(functools.partial(gradients_over, g))

    local(4).wait()
    local(2).wait()
    local(3).wait()
    n = jnp.full((8, 128), step[0] + 1, jnp.int32).astype(F32)
    scale_first = (1.0 / (1.0 - jnp.exp(n * math.log(0.9))))[0, 0]
    scale_second = (1.0 / (1.0 - jnp.exp(n * math.log(0.95))))[0, 0]

    def pieces(g, j):
        start, size = groups[g]
        for q in range(0, 2 * size, 8):
            side, r = divmod(q, size)
            rows = pl.ds(start + r, 8)
            yield q, ((0, side, rows, cols(j)), (0, 2, rows, half(j, side)))

    def adam(g, j):
        size = groups[g][1]
        first, last = gradient(d_own, h_own, g, j)
        grad[pl.ds(0, 2 * size), wide] = first
        grad[pl.ds(0, 2 * size), narrow] = last
        unit(g_send, g_recv, d_sem, z_peer, g, j).wait_recv()
        spans = (wide, narrow)
        held = {}
        for q, places in pieces(g, j):
            for span, place in zip(spans, places):
                i = 0 if span is wide else 1
                rows = pl.ds(q // 16 * 16, 16)
                if q % 16 == 0:
                    held[i] = g_recv[g][j, rows, span].astype(F32)
                theirs = held[i][q % 16: q % 16 + 8]
                gr = grad[pl.ds(q, 8), span] + theirs
                first_new = 0.9 * nm_ref[place] + 0.1 * gr
                second_new = 0.95 * nv_ref[place] + 0.05 * gr * gr
                nm_ref[place] = first_new
                nv_ref[place] = second_new
                weights = np_ref[place]
                update = first_new * scale_first / (jnp.sqrt(second_new * scale_second) + 1e-08)
                updated = weights - 0.01 * (update + 0.1 * weights)
                np_ref[place] = updated
                if q % 16 == 0:
                    held[2 + i] = updated
                else:
                    both = jnp.concatenate([held[2 + i], updated], axis=0)
                    u_send[g][j, rows, span] = both.astype(BF16)
        unit(u_send, u_recv, u_sem, after, g, j).start()

    def average(g, j):
        unit(u_send, u_recv, u_sem, after, g, j).wait_recv()
        held = {}
        for q, places in pieces(g, j):
            for i, place in enumerate(places):
                if q % 16 == 0:
                    span = (wide, narrow)[i]
                    held[i] = u_recv[g][j, pl.ds(q, 16), span].astype(F32)
                np_ref[place] = 0.5 * (np_ref[place] + held[i][q % 16: q % 16 + 8])

    def back_project(rows, j):
        total = None
        for g in range(n_groups):
            for d_ref, w in ((d_own, w_own), (d_rem, w_rem)):
                term = dot(d_ref[g][:, rows], w[g][j, :, wide], TN)
                total = term if total is None else total + term
        return total

    def input_over(j):
        return pltpu.make_async_remote_copy(
            src_ref=ig_send.at[j], dst_ref=ig_recv.at[j],
            send_sem=ig_sem.at[count], recv_sem=ig_sem.at[j],
            device_id=twin, device_id_type=MESH)

    last = n_groups - 1

    def first_pass(j):
        adam(0, j)
        gradients_over(last, j)
        ig_send[j] = back_project(other, j)
        input_over(j).start()

    def last_pass(j):
        adam(last, j)
        average(0, j)
        input_over(j).wait_recv()
        ig_ref[:, cols(j)] = (back_project(mine, j) + ig_recv[j]).astype(BF16)

        @pl.when(j >= lag)
        def _():
            average(last, j - lag)

    loop(first_pass)
    loop(last_pass)
    for g in range(n_groups):
        all_sent(w_own, w_rem, w_sem, z_peer, g)
        all_sent(g_send, g_recv, d_sem, z_peer, g)
    tokens_over(0).wait_send()
    tokens_over(1).wait_send()
    pltpu.make_async_remote_copy(
        src_ref=ig_send, dst_ref=ig_recv, send_sem=ig_sem.at[count], recv_sem=ig_sem.at[0],
        device_id=twin, device_id_type=MESH).wait_send()
    for j in range(count - lag, count):
        average(last, j)
    for g in range(n_groups):
        all_sent(u_send, u_recv, u_sem, after, g)


def window(by, collective_id, step_index, inputs, grad_out, params, first, second):
    tok, width = inputs.shape
    hid = params.shape[2]
    chunk = SEND if by == 1 else SEND // 2
    count = width // chunk
    split = hid // 16 * 8
    groups = ((0, split), (split, hid - split))
    anywhere = pl.BlockSpec(memory_space=pl.ANY)
    inside = pl.BlockSpec(memory_space=pltpu.VMEM)
    like = jax.ShapeDtypeStruct(params.shape, F32)

    def each(make):
        return [make(size) for _, size in groups]

    blocks = each(lambda n: pltpu.VMEM((count, 2 * n, chunk * 3 // 2), BF16))
    sums = each(lambda n: pltpu.VMEM((2 * n, 2 * tok), F32)) + each(
        lambda n: pltpu.VMEM((n, 2 * tok), F32))
    d_refs = each(lambda n: pltpu.VMEM((2 * n, 2 * tok), BF16))
    h_refs = each(lambda n: pltpu.VMEM((-(-n // 16) * 16, 2 * tok), BF16))
    units = pltpu.SemaphoreType.DMA((len(groups), count + 1))
    return pl.pallas_call(
        functools.partial(window_kernel, by, groups, chunk),
        out_shape=[like, like, like, jax.ShapeDtypeStruct(inputs.shape, BF16)],
        in_specs=[anywhere] * 6,
        out_specs=[inside] * 4,
        scratch_shapes=[pltpu.VMEM((2 * tok, width), BF16)] * 2
        + [pltpu.SMEM((1,), jnp.int32)]
        + [pltpu.VMEM((count, tok, chunk), F32)] * 2
        + [pltpu.VMEM((2 * hid, chunk * 3 // 2), F32)]
        + blocks * 6 + sums + d_refs * 2 + h_refs * 2
        + [units] * 4
        + [pltpu.SemaphoreType.DMA((count + 1,)), pltpu.SemaphoreType.DMA((9,))],
        compiler_params=pltpu.CompilerParams(
            collective_id=collective_id, has_side_effects=True,
            vmem_limit_bytes=40 * 2 ** 20),
        name=f"window_by_{by}",
    )(step_index, inputs, grad_out, params, first, second)


def copy_kernel(n, *refs):
    sources, targets, sem = refs[:n], refs[n: 2 * n], refs[2 * n]
    copies = []
    for source, target in zip(sources, targets):
        if len(source.shape) == 4:
            pieces = [(source.at[0, i], target.at[0, i]) for i in range(source.shape[1])]
        else:
            pieces = [(source, target)]
        for a, b in pieces:
            copies.append(pltpu.make_async_copy(a, b, sem.at[len(copies)]))
    for copy in copies:
        copy.start()
    for copy in copies:
        copy.wait()


def hand_over(arrays):
    n = len(arrays)
    anywhere = pl.BlockSpec(memory_space=pl.ANY)
    return pl.pallas_call(
        functools.partial(copy_kernel, n),
        out_shape=[jax.ShapeDtypeStruct(a.shape, a.dtype) for a in arrays],
        in_specs=[anywhere] * n,
        out_specs=[anywhere] * n,
        scratch_shapes=[pltpu.SemaphoreType.DMA((3 * n,))],
        compiler_params=pltpu.CompilerParams(vmem_limit_bytes=16 * 2 ** 20),
        name="hand_over",
    )(*arrays)


def make_branch(bit):

    def run(*values):
        return tuple(hand_over(window(1 << bit, bit, *values)))

    return run


def per_device(step_index, inputs, grad_out, params, first_moment, second_moment):
    bits = lax.axis_size("rep").bit_length() - 1
    branches = [make_branch(bit) for bit in range(bits)]
    return lax.switch(
        step_index[0] % bits, branches,
        step_index, inputs, grad_out, params, first_moment, second_moment)


def solution(mesh):
    return jax.shard_map(
        per_device,
        mesh=mesh,
        in_specs=(
            P(),
            P(("rep", "tp"), None),
            P(("rep", "tp"), None),
            P("rep", None, "tp", None),
            P("rep", None, "tp", None),
            P("rep", None, "tp", None),
        ),
        out_specs=(
            P("rep", None, "tp", None),
            P("rep", None, "tp", None),
            P("rep", None, "tp", None),
            P(("rep", "tp"), None),
        ),
        check_vma=False,
    )
```
